512 devices in a mesh: expert: 128 (over z, y, core), dp: 4 (over x).
Axes of the slice: x: 4, y: 4, z: 16, core: 2. Of those that a mesh axis runs over, the one named last changes fastest.
Arguments:
- tokens: bfloat16 [16384, 2048], P('expert', 'dp'), may hold values from -6 to 6
- grad_out: bfloat16 [16384, 2048], P('expert', 'dp'), may hold values from -6 to 6
- routes: int32 [16384, 8], P('expert'), may hold values from 0 to 127, all different within a row; in each aligned block of 128 rows (0 to 127, 128 to 255, ...) at most 12 rows name the same one
- gates: float32 [16384, 8], P('expert'), may hold values from 0.1 to 1
- w_gate: bfloat16 [128, 2048, 384], P('expert', 'dp'), may hold values from -0.125 to 0.125
- w_up: bfloat16 [128, 2048, 384], P('expert', 'dp'), may hold values from -0.125 to 0.125
- w_down: bfloat16 [128, 384, 2048], P('expert', None, 'dp'), may hold values from -0.3125 to 0.3125
Outputs:
- d_tokens: bfloat16 [16384, 2048], P('expert', 'dp')
- grad_gate: bfloat16 [128, 2048, 384], P('expert', 'dp')
- grad_up: bfloat16 [128, 2048, 384], P('expert', 'dp')
- grad_down: bfloat16 [128, 384, 2048], P('expert', None, 'dp')
The draws below stay inside these ranges and needn't reach their ends.
Inputs may be any that keep to these rules, and one draw needn't show every extreme that they name: `routes`: each row names 8 different experts; in each aligned block of 128 rows no expert is named by more than 12 rows, a bound that some block reaches.
All inputs are finite; a program needn't handle non-finite values.
Results may differ from the reference program's by a relative error of at most 0.013.
Values may be sent and summed in bfloat16 or wider, within the bound.
No kernel may reach another device: no remote copies, remote signals or barrier semaphores. Data moves between devices by JAX's collectives and lax.ppermute only.
A program may use at most 64 MiB of HBM per device.

```python
import math
import jax
import jax.numpy as jnp
import numpy as np
from jax import lax

D = 2048
TOP = 8
FW = 384
TOK_DEV = 128
EXPERTS = 128
MOST = 12
TOKENS = 16384
N_EXPERT = 128
N_DP = 4


def steps_of(stream_key, extent, split, least, largest):
    level, own = 1.0, jax.random.fold_in(stream_key, 6)
    for dim, parts in split:
        heights = jnp.exp(jax.random.uniform(jax.random.fold_in(own, dim), (parts,), jnp.float32, least / len(split), largest / len(split)))
        level = level * jnp.repeat(heights, extent[dim] // parts).reshape([-1 if axis == dim else 1 for axis in range(len(extent))])
    return level


def assign_block(stream_key, own, number, rows, count, top, bound, skew):
    order = jax.random.permutation(stream_key, count)
    crowded, common = load_shares(count, rows * top, bound, skew, True), load_shares(count, rows * top, bound, skew, False)
    places = jnp.arange(count)

    def named(sizes, turn):
        used = int((sizes > 0).sum())
        fixed = max(1, used // 4)
        moved = fixed + (places - fixed + turn * (used - fixed)) % max(1, count - fixed)
        return jnp.zeros((count,), jnp.int32).at[order[jnp.where(places < fixed, places, moved)]].set(jnp.asarray(sizes, jnp.int32))

    sizes = jnp.where(number % 4 == 0, named(crowded, number // 4), named(common, number - number // 4 - 1))
    mixed = jax.random.permutation(jax.random.fold_in(own, 3), count)
    giver, sink = mixed[0:count // 2 * 2:2], mixed[1:count // 2 * 2:2]
    room = jnp.minimum(sizes[giver] - 1, bound - sizes[sink]) // 2
    room = jnp.where((giver == order[0]) | (sink == order[0]) | (sizes[sink] == 0), 0, jnp.maximum(room, 0))
    moved = jax.random.randint(jax.random.fold_in(own, 4), (count // 2,), 0, 1 << 20) % (room + 1)
    sizes = sizes.at[giver].add(-moved).at[sink].add(moved)
    members = jnp.searchsorted(jnp.cumsum(sizes), jnp.arange(rows * top), side="right").astype(jnp.int32)
    table = members.reshape(top, rows).T
    table = table[jax.random.permutation(jax.random.fold_in(own, 1), rows)]
    turn = jax.random.randint(jax.random.fold_in(own, 2), (rows, 1), 0, top)
    return jnp.take_along_axis(table, (jnp.arange(top)[None, :] + turn) % top, axis=1)


def load_shares(count, total, most, slope, full):
    loads = [(1 << 20) // math.isqrt(rank ** slope) + 1 for rank in range(1, count + 1)]
    largest = most if full else min(most, max(-(-total // count), total * loads[0] // sum(loads)))
    least = 1 if total - largest >= count - 1 else 0
    holding, rest = [largest] + [least] * (count - 1), total - largest - least * (count - 1)
    while rest > 0:
        candidates = [i for i in range(1, count) if holding[i] < largest] or [i for i in range(1, count) if holding[i] < most]
        whole, budget = sum([loads[i] for i in candidates]), rest
        for i in candidates:
            addition = min(most - holding[i], max(1, budget * loads[i] // whole), rest)
            holding[i] = holding[i] + addition
            rest = rest - addition
    return np.array(holding)


def scatter_about(stream_key, dims, scale, bound, shards=(), kind=jnp.bfloat16):
    level = steps_of(stream_key, dims, shards, -0.22, 0.18) if shards else 1.0
    result = jax.random.normal(stream_key, dims, jnp.float32) * scale * level
    return jnp.minimum(jnp.maximum(result, -bound), bound).astype(kind)


def setup_inputs(seed: int = 0) -> dict:
    keys = jax.random.split(jax.random.key(seed), 8)
    tokens = scatter_about(keys[0], (TOKENS, D), 1.0, 6.0, ((0, 128), (1, 4)))
    grad_out = scatter_about(keys[1], (TOKENS, D), 1.0, 6.0, ((0, 128), (1, 4)))
    routes_keys = jax.random.split(jax.random.fold_in(keys[2], 1), TOKENS // TOK_DEV)
    routes_turns = jax.random.permutation(jax.random.fold_in(keys[2], 3), TOKENS // TOK_DEV)
    routes = jax.vmap(lambda own, number: assign_block(jax.random.fold_in(keys[2], 2), own, number, TOK_DEV, EXPERTS, TOP, MOST, 2))(routes_keys, routes_turns).reshape((TOKENS, TOP))
    gates = jnp.clip(jnp.exp(math.log(1.0) - 2.3025851 * jax.random.uniform(keys[3], (TOKENS, TOP), jnp.float32) ** steps_of(keys[3], (TOKENS, TOP), ((0, 128),), -0.2, 0.2)), 0.1, 1.0)
    w_gate = scatter_about(keys[4], (EXPERTS, D, FW), D ** -0.5, 0.125, ((0, 128), (1, 4)))
    w_up = scatter_about(keys[5], (EXPERTS, D, FW), D ** -0.5, 0.125, ((0, 128), (1, 4)))
    w_down = scatter_about(keys[6], (EXPERTS, FW, D), FW ** -0.5, 0.3125, ((0, 128), (2, 4)))
    return {"tokens": tokens, "grad_out": grad_out, "routes": routes, "gates": gates, "w_gate": w_gate, "w_up": w_up, "w_down": w_down}


def split_round(left_rows, right_rows, member):
    masked = right_rows.astype(jnp.float32)[None, :, :] * member.T[:, :, None]
    partial_value = jnp.einsum("ra,jrb->jab", left_rows.astype(jnp.float32), masked)
    rounded = lax.optimization_barrier(partial_value.astype(jnp.bfloat16))
    return jnp.sum(rounded.astype(jnp.float32), axis=0).astype(jnp.bfloat16)


def reference(tokens, grad_out, routes, gates, w_gate, w_up, w_down):
    flat_routes = routes.reshape(-1).astype(jnp.int32)
    flat_gates = gates.reshape(-1)
    row_total = TOKENS * TOP
    capacity = N_EXPERT * MOST
    model_width = tokens.shape[1]
    group_width = N_EXPERT // N_DP

    def one_expert(accum, expert_id):
        found = jnp.nonzero(flat_routes == expert_id, size=capacity, fill_value=row_total)[0].astype(jnp.int32)
        valid = found < row_total
        safe_rows = jnp.where(valid, found, 0).astype(jnp.int32)
        token_ids = (safe_rows // TOP).astype(jnp.int32)
        replica = ((token_ids // TOK_DEV) // group_width).astype(jnp.int32)
        member = ((replica[:, None] == jnp.arange(N_DP, dtype=jnp.int32)[None, :]) & valid[:, None]).astype(jnp.float32)
        inputs = jnp.where(valid[:, None], tokens[token_ids], jnp.zeros((), tokens.dtype))
        scaled = jnp.where(valid[:, None], grad_out[token_ids].astype(jnp.float32) * flat_gates[safe_rows][:, None], 0.0).astype(jnp.bfloat16)
        wg = w_gate[expert_id]
        wu = w_up[expert_id]
        wd = w_down[expert_id]
        pre_gate = jnp.dot(inputs, wg, preferred_element_type=jnp.float32)
        pre_up = jnp.dot(inputs, wu, preferred_element_type=jnp.float32)
        sigmoid_gate = jax.nn.sigmoid(pre_gate)
        activated = pre_gate * sigmoid_gate
        hidden = (activated * pre_up).astype(jnp.bfloat16)
        back_hidden = jnp.dot(scaled, wd.T, preferred_element_type=jnp.float32)
        d_up = (back_hidden * activated).astype(jnp.bfloat16)
        d_gate = (back_hidden * pre_up * sigmoid_gate * (1.0 + pre_gate * (1.0 - sigmoid_gate))).astype(jnp.bfloat16)
        row_grad = (jnp.dot(d_gate, wg.T, preferred_element_type=jnp.float32) + jnp.dot(d_up, wu.T, preferred_element_type=jnp.float32)).astype(jnp.bfloat16)
        contrib = jnp.where(valid[:, None], row_grad.astype(jnp.float32), 0.0)
        accum = accum.at[token_ids].add(contrib)
        grads = (split_round(inputs, d_gate, member), split_round(inputs, d_up, member), split_round(hidden, scaled, member))
        return accum, grads

    start = jnp.zeros((TOKENS, model_width), jnp.float32)
    accum, grads = lax.scan(one_expert, start, jnp.arange(EXPERTS, dtype=jnp.int32))
    return accum.astype(jnp.bfloat16), grads[0], grads[1], grads[2]
```

```python
import jax
import jax.numpy as jnp
from jax import lax
from jax.sharding import Mesh
from jax.sharding import PartitionSpec as P

MOST = 12
N_Z, N_Y, N_C, N_X = 16, 4, 2, 4
PLANE = ("x", "y", "c")
F32 = jnp.float32
BF16 = jnp.bfloat16


def dot(left, right, contract, batch=((), ())):
    return lax.dot_general(left, right, (contract, batch), preferred_element_type=F32)


def shift(value, by):
    return lax.ppermute(value, "x", [(i, (i + by) % N_X) for i in range(N_X)])


def gather_x(value, me):
    whole = jnp.zeros((N_X,) + value.shape, value.dtype)
    for by in range(N_X):
        piece = value if by == 0 else shift(value, by)
        whole = lax.dynamic_update_slice_in_dim(whole, piece[None], (me - by) % N_X, 0)
    return whole


def plan(routes, gates, me_z):
    tok = routes.shape[0]
    mine = jnp.concatenate([routes.T.astype(F32), gates.T], axis=0)
    every = lax.all_to_all(
        jnp.broadcast_to(mine[None], (N_Z,) + mine.shape), "z", split_axis=0, concat_axis=0, tiled=True
    )
    top = routes.shape[1]
    near = N_Y * N_C
    named = every[:, :top].reshape(N_Z, top, 1, tok)
    weight = every[:, top:].reshape(N_Z, top, 1, tok)
    wanted = (me_z * near + jnp.arange(near, dtype=jnp.int32)).astype(F32)
    hit = named == wanted[None, None, :, None]
    member = jnp.sum(hit.astype(F32), axis=1)
    gate = jnp.sum(jnp.where(hit, weight, 0.0), axis=1)
    before = (jnp.arange(tok)[:, None] < jnp.arange(tok)[None, :]).astype(BF16)
    rank = dot(member.astype(BF16), before, ((2,), (0,)))
    within = (jnp.arange(N_Z) % (N_Z // N_X) * MOST).astype(F32)
    slot = jnp.where(member > 0.5, rank + within[:, None, None], -1.0)

    def by_group(value):
        value = value.reshape(N_X, N_Z // N_X, near, tok)
        return value.transpose(0, 2, 1, 3).reshape(N_X, near, 1, N_Z // N_X * tok)

    slots = N_Z // N_X * MOST
    pick = by_group(slot) == jnp.arange(slots, dtype=jnp.int32).astype(F32)[None, None, :, None]
    row_gate = jnp.sum(jnp.where(pick, by_group(gate), 0.0), axis=3)
    return (
        pick.astype(BF16).reshape(N_X, near * slots, N_Z // N_X * tok),
        row_gate.reshape(N_X, near * slots, 1),
    )


def shards(tokens, grad_out, routes, gates, w_gate, w_up, w_down):
    me_z, me_x = lax.axis_index("z"), lax.axis_index("x")
    tok, cols = tokens.shape
    both = jnp.concatenate([tokens, grad_out], axis=1)
    column = lax.all_gather(both, "z", axis=0, tiled=True).reshape(N_X, N_Z // N_X * tok, 2 * cols)
    pick, row_gate = plan(routes, gates, me_z)
    full_gate = gather_x(w_gate[0], me_x)
    full_up = gather_x(w_up[0], me_x)
    full_down = gather_x(w_down[0], me_x)

    rows = dot(pick, column, ((2,), (1,)), ((0,), (0,)))
    scale = jnp.where(jnp.arange(2 * cols)[None, None, :] < cols, 1.0, row_gate)
    rows = (rows * scale).astype(BF16)
    count = rows.shape[1]
    slots = count // (N_Y * N_C)
    rows = lax.all_to_all(
        rows.reshape(-1, slots, 2 * cols), PLANE, split_axis=0, concat_axis=0, tiled=True
    ).reshape(N_X, count, 2 * cols)
    inputs, scaled = rows[:, :, :cols], rows[:, :, cols:]

    def over_features(left, right, axis):
        return sum(dot(left[j], right[j], ((1,), (axis,))) for j in range(N_X))

    pre_gate = over_features(inputs, full_gate, 0)
    pre_up = over_features(inputs, full_up, 0)
    back_hidden = over_features(scaled, full_down, 1)
    sigmoid_gate = jax.nn.sigmoid(pre_gate)
    activated = pre_gate * sigmoid_gate
    hidden = (activated * pre_up).astype(BF16)
    d_up = (back_hidden * activated).astype(BF16)
    d_gate = (back_hidden * pre_up * sigmoid_gate * (1.0 + pre_gate * (1.0 - sigmoid_gate))).astype(BF16)

    row_grad = jnp.stack(
        [
            (dot(d_gate, full_gate[j], ((1,), (1,))) + dot(d_up, full_up[j], ((1,), (1,)))).astype(BF16)
            for j in range(N_X)
        ]
    )
    came_back = lax.all_to_all(
        row_grad.reshape(-1, slots, cols), PLANE, split_axis=0, concat_axis=0, tiled=True
    ).reshape(N_X, count, cols)
    token_grad = dot(pick, came_back, ((1,), (1,)), ((0,), (0,))).astype(BF16)
    d_tokens = lax.psum_scatter(token_grad.reshape(-1, cols), "z", scatter_dimension=0, tiled=True)

    totals = [None, None, None]
    for by in (1, 3, 2, 0):
        to = (me_x + by) % N_X
        ins = lax.dynamic_index_in_dim(inputs, to, 0, keepdims=False)
        outs = lax.dynamic_index_in_dim(scaled, to, 0, keepdims=False)
        for k, (left, right) in enumerate(((ins, d_gate), (ins, d_up), (hidden, outs))):
            part = dot(left, right, ((0,), (0,))).astype(BF16)
            part = (shift(part, by) if by else part).astype(F32)
            totals[k] = part if totals[k] is None else totals[k] + part
    grads = [total.astype(BF16)[None] for total in totals]
    return (d_tokens, *grads)


def solution(mesh):
    fine = Mesh(mesh.devices.reshape(N_Z, N_Y, N_C, N_X), ("z", "y", "c", "x"))
    expert = ("z", "y", "c")
    return jax.shard_map(
        shards,
        mesh=fine,
        in_specs=(
            P(expert, "x"),
            P(expert, "x"),
            P(expert, None),
            P(expert, None),
            P(expert, "x", None),
            P(expert, "x", None),
            P(expert, None, "x"),
        ),
        out_specs=(
            P(expert, "x"),
            P(expert, "x", None),
            P(expert, "x", None),
            P(expert, None, "x"),
        ),
        check_vma=False,
    )
```

```python
import jax
import jax.numpy as jnp
from jax import lax
from jax.experimental import pallas as pl
from jax.experimental.pallas import tpu as pltpu
from jax.sharding import Mesh
from jax.sharding import PartitionSpec as P

MOST = 12
N_FAR, N_NEAR, N_Y, N_C, N_X = 8, 2, 4, 2, 4
PLANE = ("x", "near", "y", "c")
LOCAL = N_NEAR * N_Y * N_C
GROUP = N_FAR // N_X
F32 = jnp.float32
BF16 = jnp.bfloat16


def dot(left, right, contract, batch=((), ())):
    return lax.dot_general(left, right, (contract, batch), preferred_element_type=F32)


def shift(value, by):
    return lax.ppermute(value, "x", [(i, (i + by) % N_X) for i in range(N_X)])


def gather_x(value, me):
    whole = jnp.zeros((N_X,) + value.shape, value.dtype)
    for by in range(N_X):
        piece = value if by == 0 else shift(value, by)
        whole = lax.dynamic_update_slice_in_dim(whole, piece[None], (me - by) % N_X, 0)
    return whole


def plan(routes, gates, me_far):
    tok, top = routes.shape
    mine = jnp.concatenate([routes.T.astype(F32), gates.T], axis=0)
    every = lax.all_to_all(
        jnp.broadcast_to(mine[None], (N_FAR,) + mine.shape), "far", split_axis=0, concat_axis=0, tiled=True
    )
    named = every[:, :top].reshape(N_FAR, top, 1, tok)
    weight = every[:, top:].reshape(N_FAR, top, 1, tok)
    wanted = (me_far * LOCAL + jnp.arange(LOCAL, dtype=jnp.int32)).astype(F32)
    hit = named == wanted[None, None, :, None]
    member = jnp.sum(hit.astype(F32), axis=1)
    gate = jnp.sum(jnp.where(hit, weight, 0.0), axis=1)
    before = (jnp.arange(tok)[:, None] < jnp.arange(tok)[None, :]).astype(BF16)
    rank = dot(member.astype(BF16), before, ((2,), (0,)))
    within = (jnp.arange(N_FAR) % GROUP * MOST).astype(F32)
    slot = jnp.where(member > 0.5, rank + within[:, None, None], -1.0)

    def by_group(value):
        value = value.reshape(N_X, GROUP, LOCAL, tok)
        return value.transpose(0, 2, 1, 3).reshape(N_X, LOCAL, 1, GROUP * tok)

    slots = GROUP * MOST
    pick = by_group(slot) == jnp.arange(slots, dtype=jnp.int32).astype(F32)[None, None, :, None]
    row_gate = jnp.sum(jnp.where(pick, by_group(gate), 0.0), axis=3)
    return (
        pick.astype(BF16).reshape(N_X, LOCAL * slots, GROUP * tok),
        row_gate.reshape(N_X, LOCAL * slots, 1),
    )


def expert_kernel(rows, both_in, down, row_grad, hidden, d_gate, d_up, pre_gate, pre_up, back):
    step = pl.program_id(0)
    width, cols = down.shape[1:]

    @pl.when(step == 0)
    def _():
        pre_gate[...] = jnp.zeros_like(pre_gate)
        pre_up[...] = jnp.zeros_like(pre_up)
        back[...] = jnp.zeros_like(back)

    ins = rows[0, :, :cols]
    pre_gate[...] += dot(ins, both_in[step, :, :width], ((1,), (0,)))
    pre_up[...] += dot(ins, both_in[step, :, width:], ((1,), (0,)))
    back[...] += dot(rows[0, :, cols:], down[0], ((1,), (1,)))

    @pl.when(step == N_X - 1)
    def _():
        g, u, b = pre_gate[...], pre_up[...], back[...]
        s = jax.nn.sigmoid(g)
        activated = g * s
        hidden[...] = (activated * u).astype(BF16)
        du = (b * activated).astype(BF16)
        dg = (b * u * s * (1.0 + g * (1.0 - s))).astype(BF16)
        d_up[...] = du
        d_gate[...] = dg
        for j in range(N_X):
            from_gate = dot(dg, both_in[j, :, :width], ((1,), (1,)))
            from_up = dot(du, both_in[j, :, width:], ((1,), (1,)))
            row_grad[j] = (from_gate + from_up).astype(BF16)


def expert(rows, both_in, down):
    parts, count, both = rows.shape
    width, cols = down.shape[1:]
    whole = lambda shape: pl.BlockSpec(shape, lambda j: (0,) * len(shape))
    square = jax.ShapeDtypeStruct((count, width), BF16)
    return pl.pallas_call(
        expert_kernel,
        grid=(parts,),
        in_specs=[
            pl.BlockSpec((1, count, both), lambda j: (j, 0, 0)),
            whole(both_in.shape),
            pl.BlockSpec((1, width, cols), lambda j: (j, 0, 0)),
        ],
        out_specs=[whole((parts, count, cols)), *[whole((count, width))] * 3],
        out_shape=[jax.ShapeDtypeStruct((parts, count, cols), BF16), square, square, square],
        scratch_shapes=[pltpu.VMEM((count, width), F32)] * 3,
        compiler_params=pltpu.CompilerParams(
            dimension_semantics=("arbitrary",), vmem_limit_bytes=32 * 1024 * 1024
        ),
        cost_estimate=pl.CostEstimate(
            flops=10 * parts * count * cols * width, bytes_accessed=11_000_000, transcendentals=count * width
        ),
    )(rows, both_in, down)


def shards(tokens, grad_out, routes, gates, w_gate, w_up, w_down):
    me_far, me_x = lax.axis_index("far"), lax.axis_index("x")
    tok, cols = tokens.shape
    both = jnp.concatenate([tokens, grad_out], axis=1)
    w_in = jnp.concatenate([w_gate[0], w_up[0]], axis=1)
    both, w_in, w_down = lax.optimization_barrier((both, w_in, w_down[0]))
    column = lax.all_gather(both, "far", axis=0, tiled=True).reshape(N_X, GROUP * tok, 2 * cols)
    pick, row_gate = plan(routes, gates, me_far)
    full_in = gather_x(w_in, me_x)
    full_down = gather_x(w_down, me_x)
    column, full_in, full_down = lax.optimization_barrier((column, full_in, full_down))

    rows = dot(pick, column, ((2,), (1,)), ((0,), (0,)))
    scale = jnp.where(jnp.arange(2 * cols)[None, None, :] < cols, 1.0, row_gate)
    rows = (rows * scale).astype(BF16)
    count = rows.shape[1]
    slots = count // LOCAL
    rows = lax.all_to_all(
        rows.reshape(-1, slots, 2 * cols), PLANE, split_axis=0, concat_axis=0, tiled=True
    ).reshape(N_X, count, 2 * cols)
    inputs, scaled = rows[:, :, :cols], rows[:, :, cols:]
    row_grad, hidden, d_gate, d_up = expert(rows, full_in, full_down)
    came_back = lax.all_to_all(
        row_grad.reshape(-1, slots, cols), PLANE, split_axis=0, concat_axis=0, tiled=True
    ).reshape(N_X, count, cols)
    token_grad = dot(pick, came_back, ((1,), (1,)), ((0,), (0,))).astype(BF16)
    d_tokens = lax.psum_scatter(token_grad.reshape(-1, cols), "far", scatter_dimension=0, tiled=True)

    totals = [None, None, None]
    for by in (1, 3, 2, 0):
        to = (me_x + by) % N_X
        ins = lax.dynamic_index_in_dim(inputs, to, 0, keepdims=False)
        outs = lax.dynamic_index_in_dim(scaled, to, 0, keepdims=False)
        for k, (left, right) in enumerate(((ins, d_gate), (ins, d_up), (hidden, outs))):
            part = dot(left, right, ((0,), (0,))).astype(BF16)
            part = (shift(part, by) if by else part).astype(F32)
            totals[k] = part if totals[k] is None else totals[k] + part
    grads = [total.astype(BF16)[None] for total in totals]
    return (d_tokens, *grads)


def solution(mesh):
    sizes = (N_FAR, N_NEAR, N_Y, N_C, N_X)
    fine = Mesh(mesh.devices.reshape(sizes), ("far", "near", "y", "c", "x"))
    expert_axes = ("far", "near", "y", "c")
    return jax.shard_map(
        shards,
        mesh=fine,
        in_specs=(
            P(expert_axes, "x"),
            P(expert_axes, "x"),
            P(expert_axes, None),
            P(expert_axes, None),
            P(expert_axes, "x", None),
            P(expert_axes, "x", None),
            P(expert_axes, None, "x"),
        ),
        out_specs=(
            P(expert_axes, "x"),
            P(expert_axes, "x", None),
            P(expert_axes, "x", None),
            P(expert_axes, None, "x"),
        ),
        check_vma=False,
    )
```

```python
import functools

import jax
import jax.numpy as jnp
from jax import lax
from jax.experimental import pallas as pl
from jax.experimental.pallas import tpu as pltpu
from jax.sharding import Mesh
from jax.sharding import PartitionSpec as P

MOST = 12
TILE = 128
N_FAR, N_NEAR, N_Y, N_C, N_X = 8, 2, 4, 2, 4
PLANE = ("x", "near", "y", "c")
LOCAL = N_NEAR * N_Y * N_C
GROUP = N_FAR // N_X
F32 = jnp.float32
BF16 = jnp.bfloat16


def dot(left, right, contract, batch=((), ())):
    return lax.dot_general(left, right, (contract, batch), preferred_element_type=F32)


def hop(value, by):
    return lax.ppermute(value, "far", [(i, (i + by) % N_FAR) for i in range(N_FAR)])


def ring_gather(value, me):
    half = value.shape[0] // 32 * 16
    whole = jnp.zeros((N_FAR,) + value.shape, value.dtype)

    def put(whole, block, by, row=0):
        return lax.dynamic_update_slice(whole, block[None], ((me + by) & (N_FAR - 1), row, 0))

    whole = put(whole, value, 0)
    up = down = value
    for step in range(1, N_FAR // 2):
        up, down = hop(up, 1), hop(down, -1)
        whole = put(put(whole, up, -step), down, step)
    up, down = hop(up[:half], 1), hop(down[half:], -1)
    return put(put(whole, up, N_FAR // 2), down, N_FAR // 2, half)


def choices(routes, gates):
    high = lax.reduce_precision(gates, 8, 7)
    mid = lax.reduce_precision(gates - high, 8, 7)
    low = gates - high - mid
    kinds = [value.T.astype(BF16) for value in (routes.astype(F32), high, mid, low)]
    rows = jnp.concatenate(kinds, axis=1)
    return jnp.pad(rows, ((0, 16 - rows.shape[0]), (0, 0)))


def pick_kernel(me, tokens, cotangents, rows, pick, *, top):
    tok, cols = cotangents.shape[1:]
    count = rows.shape[1]
    slots = GROUP * MOST
    before = lax.broadcasted_iota(jnp.int32, (tok, tok), 0) < lax.broadcasted_iota(jnp.int32, (tok, tok), 1)
    before = before.astype(F32).astype(BF16)
    wanted = (lax.broadcasted_iota(jnp.int32, (LOCAL, tok), 0) + me[0] * LOCAL).astype(F32)
    slot, gate = [], []
    for u in range(GROUP):
        choice = tokens[u, tok:, :].astype(F32)
        member = jnp.zeros((LOCAL, tok), F32)
        chosen = jnp.zeros((LOCAL, tok), F32)
        for k in range(top):
            kinds = [choice[k : k + 1, tok * i : tok * (i + 1)] for i in range(4)]
            hit = kinds[0] == wanted
            member = jnp.where(hit, 1.0, member)
            chosen = jnp.where(hit, kinds[1] + kinds[2] + kinds[3], chosen)
        rank = dot(member.astype(BF16), before, ((1,), (0,)))
        slot.append(jnp.where(member > 0.5, rank + float(MOST * u), -1.0))
        gate.append(chosen)
    slot, gate = jnp.concatenate(slot, axis=1), jnp.concatenate(gate, axis=1)
    place = lax.broadcasted_iota(jnp.int32, (LOCAL, slots, GROUP * tok), 1).astype(F32)
    hit = slot[:, None, :] == place
    onehot = jnp.where(hit, 1.0, 0.0).reshape(count, GROUP * tok).astype(BF16)
    row_gate = jnp.where(hit, gate[:, None, :], 0.0).reshape(count, GROUP * tok)
    row_gate = jnp.sum(row_gate, axis=1, keepdims=True)
    pick[0] = onehot

    def select(blocks):
        return sum(
            dot(onehot[:, tok * u : tok * (u + 1)], blocks[u, :tok, :], ((1,), (0,))) for u in range(GROUP)
        )

    rows[0, :, :cols] = select(tokens).astype(BF16)
    rows[0, :, cols:] = (select(cotangents) * row_gate).astype(BF16)


def pick_rows(me, tokens, cotangents, top):
    tok, cols = cotangents.shape[1:]
    count = LOCAL * GROUP * MOST
    grouped = lambda shape: pl.BlockSpec(shape, lambda i: (i, 0, 0))
    return pl.pallas_call(
        functools.partial(pick_kernel, top=top),
        grid=(N_X,),
        in_specs=[
            pl.BlockSpec(memory_space=pltpu.SMEM),
            grouped((GROUP,) + tokens.shape[1:]),
            grouped((GROUP, tok, cols)),
        ],
        out_specs=[grouped((1, count, 2 * cols)), grouped((1, count, GROUP * tok))],
        out_shape=[
            in_hbm(N_X, count, 2 * cols),
            in_hbm(N_X, count, GROUP * tok),
        ],
        compiler_params=params(),
        cost_estimate=pl.CostEstimate(
            flops=4 * N_X * count * GROUP * tok * cols, bytes_accessed=7_000_000, transcendentals=0
        ),
    )(me[None], tokens, cotangents)


def expert_kernel(rows, w_in, w_out, row_grad, backs, hidden, pre_gate, pre_up, back):
    step = pl.program_id(0)
    cols = row_grad.shape[2]
    width = hidden.shape[1]

    @pl.when(step == 0)
    def _():
        pre_gate[...] = jnp.zeros_like(pre_gate)
        pre_up[...] = jnp.zeros_like(pre_up)
        back[...] = jnp.zeros_like(back)

    ins = rows[0, :, :cols]
    pre_gate[...] += dot(ins, w_in[step, :, :width], ((1,), (0,)))
    pre_up[...] += dot(ins, w_in[step, :, width:], ((1,), (0,)))
    back[...] += dot(rows[0, :, cols:], w_out[0], ((1,), (1,)))

    @pl.when(step == N_X - 1)
    def _():
        g, u, b = pre_gate[...], pre_up[...], back[...]
        s = jax.nn.sigmoid(g)
        activated = g * s
        hidden[...] = (activated * u).astype(BF16)
        d_up = (b * activated).astype(BF16)
        d_gate = (b * u * s * (1.0 + g * (1.0 - s))).astype(BF16)
        backs[:, :width] = d_gate
        backs[:, width:] = d_up
        for j in range(N_X):
            from_gate = dot(d_gate, w_in[j, :, :width], ((1,), (1,)))
            from_up = dot(d_up, w_in[j, :, width:], ((1,), (1,)))
            row_grad[j] = (from_gate + from_up).astype(BF16)


def whole(shape):
    return pl.BlockSpec(shape, lambda *_: (0,) * len(shape))


def params():
    return pltpu.CompilerParams(dimension_semantics=("arbitrary",), vmem_limit_bytes=32 * 1024 * 1024)


def in_hbm(*shape):
    return pltpu.HBM(shape, BF16)


def expert(rows, w_in, w_out):
    parts, count, both = rows.shape
    width, cols = w_out.shape[1:]
    shapes = (parts, count, cols), (count, 2 * width), (count, width)
    return pl.pallas_call(
        expert_kernel,
        grid=(parts,),
        in_specs=[
            pl.BlockSpec((1, count, both), lambda j: (j, 0, 0)),
            whole(w_in.shape),
            pl.BlockSpec((1, width, cols), lambda j: (j, 0, 0)),
        ],
        out_specs=[whole(shape) for shape in shapes],
        out_shape=[in_hbm(*shapes[0]), *[jax.ShapeDtypeStruct(shape, BF16) for shape in shapes[1:]]],
        scratch_shapes=[pltpu.VMEM((count, width), F32)] * 3,
        compiler_params=params(),
        cost_estimate=pl.CostEstimate(
            flops=10 * parts * count * cols * width, bytes_accessed=11_000_000, transcendentals=count * width
        ),
    )(rows, w_in, w_out)


def tiles(height, breadth, wide):
    for n in range(height * breadth // TILE**2):
        there, here = divmod(n, wide // TILE), divmod(n, breadth // TILE)
        yield tuple(pl.ds(TILE * i, TILE) for i in here), tuple(TILE * i for i in there)


def parts_kernel(rows, backs, hidden, out, down):
    cols = rows.shape[2] // 2
    out[0, :cols] = dot(rows[0, :, :cols], backs[...], ((0,), (0,))).astype(BF16)
    down[...] = dot(hidden[...], rows[0, :, cols:], ((0,), (0,)))
    for here, there in tiles(*down.shape, out.shape[2]):
        out[0, cols + there[0] : cols + there[0] + TILE, there[1] : there[1] + TILE] = down[here].astype(BF16)


def weight_parts(rows, backs, hidden):
    parts, count, both = rows.shape
    cols, width, wide = both // 2, hidden.shape[1], backs.shape[1]
    shape = parts, cols + width * cols // wide, wide
    return pl.pallas_call(
        parts_kernel,
        grid=(parts,),
        in_specs=[
            pl.BlockSpec((1, count, both), lambda j: (j, 0, 0)),
            whole(backs.shape),
            whole(hidden.shape),
        ],
        out_specs=pl.BlockSpec((1, *shape[1:]), lambda j: (j, 0, 0)),
        out_shape=in_hbm(*shape),
        scratch_shapes=[pltpu.VMEM((width, cols), F32)],
        compiler_params=params(),
        cost_estimate=pl.CostEstimate(
            flops=parts * count * both * width * 3, bytes_accessed=9_000_000, transcendentals=0
        ),
    )(rows, backs, hidden)


def unpack_kernel(sums, gate, up, down):
    cols, width = gate.shape
    gate[...] = sums[:cols, :width]
    up[...] = sums[:cols, width:]
    for here, there in tiles(*down.shape, sums.shape[1]):
        down[here] = sums[cols + there[0] : cols + there[0] + TILE, there[1] : there[1] + TILE]


def unpack(sums, cols, width):
    shapes = (cols, width), (cols, width), (width, cols)
    return pl.pallas_call(
        unpack_kernel,
        out_shape=[jax.ShapeDtypeStruct(shape, BF16) for shape in shapes],
        compiler_params=pltpu.CompilerParams(vmem_limit_bytes=32 * 1024 * 1024),
        cost_estimate=pl.CostEstimate(flops=0, bytes_accessed=2_400_000, transcendentals=0),
    )(sums)


def tokens_kernel(me, pick, back, own, up, down, two):
    tok = own.shape[1]
    for target, steps in ((up, (1, 5)), (down, (7, 3)), (two, (2, 6)), (own, (0, 4))):
        for place, step in enumerate(steps):
            far = lax.rem(me[0] + step, N_FAR)
            group, within = lax.div(far, GROUP), lax.rem(far, GROUP)
            chosen = pick[group, :, pl.ds(pl.multiple_of(within * tok, tok), tok)]
            target[place] = dot(chosen, back[group], ((0,), (0,))).astype(BF16)


def token_parts(me, pick, back):
    tok = pick.shape[2] // GROUP
    pair = (2, tok, back.shape[2])
    return pl.pallas_call(
        tokens_kernel,
        in_specs=[pl.BlockSpec(memory_space=pltpu.SMEM)] + [pl.BlockSpec(memory_space=pltpu.VMEM)] * 2,
        out_specs=[pl.BlockSpec(memory_space=pltpu.VMEM)] * 4,
        out_shape=[jax.ShapeDtypeStruct(pair, BF16)] * 4,
        compiler_params=pltpu.CompilerParams(vmem_limit_bytes=32 * 1024 * 1024),
        cost_estimate=pl.CostEstimate(
            flops=2 * back.size * tok * GROUP, bytes_accessed=4_000_000, transcendentals=0
        ),
    )(me[None], pick, back)


def scatter_sum(me, pick, back):
    own, up, down, two = token_parts(me, pick, back)
    half = own.shape[2] // 2
    up, down = hop(up, 1), hop(down, -1)
    left, right = hop(two[:, :, :half], 2), hop(two[::-1, :, half:], -2)
    total = own.astype(F32) + up.astype(F32) + down.astype(F32)
    total = total + jnp.concatenate([left, right], axis=2).astype(F32)
    opposite = hop(total[1].astype(BF16), N_FAR // 2)
    return (total[0] + opposite.astype(F32)).astype(BF16)


def shards(tokens, grad_out, routes, gates, w_gate, w_up, w_down):
    me_far = lax.axis_index("far")
    cols = tokens.shape[1]
    width = w_gate.shape[2]
    w_in = lax.all_gather(jnp.concatenate([w_gate[0], w_up[0]], axis=1), "x", axis=0)
    w_out = lax.all_gather(w_down[0], "x", axis=0)
    marked = jnp.concatenate([tokens, choices(routes, gates)], axis=0)
    cotangents = ring_gather(grad_out, me_far)
    marked = ring_gather(marked, me_far)
    w_in, marked, cotangents = lax.optimization_barrier((w_in, marked, cotangents))
    rows, pick = pick_rows(me_far, marked, cotangents, routes.shape[1])
    count = rows.shape[1]
    slots = count // LOCAL
    rows = lax.all_to_all(
        rows.reshape(-1, slots, 2 * cols), PLANE, split_axis=0, concat_axis=0, tiled=True
    ).reshape(N_X, count, 2 * cols)
    row_grad, backs, hidden = expert(rows, w_in, w_out)
    came_back = lax.all_to_all(
        row_grad.reshape(-1, slots, cols), PLANE, split_axis=0, concat_axis=0, tiled=True
    ).reshape(N_X, count, cols)
    parts = weight_parts(rows, backs, hidden)
    grads = lax.psum_scatter(parts, "x", scatter_dimension=0, tiled=False)
    d_tokens = scatter_sum(me_far, pick, came_back)
    grads = unpack(grads, cols, width)
    return (d_tokens, *[grad[None] for grad in grads])


def solution(mesh):
    sizes = (N_FAR, N_NEAR, N_Y, N_C, N_X)
    fine = Mesh(mesh.devices.reshape(sizes), ("far", "near", "y", "c", "x"))
    expert_axes = ("far", "near", "y", "c")
    return jax.shard_map(
        shards,
        mesh=fine,
        in_specs=(
            P(expert_axes, "x"),
            P(expert_axes, "x"),
            P(expert_axes, None),
            P(expert_axes, None),
            P(expert_axes, "x", None),
            P(expert_axes, "x", None),
            P(expert_axes, None, "x"),
        ),
        out_specs=(
            P(expert_axes, "x"),
            P(expert_axes, "x", None),
            P(expert_axes, "x", None),
            P(expert_axes, None, "x"),
        ),
        check_vma=False,
    )
```

```python
import jax
import jax.numpy as jnp
from jax import lax
from jax.experimental import pallas as pl
from jax.experimental.pallas import tpu as pltpu
from jax.sharding import Mesh
from jax.sharding import PartitionSpec as P

MOST = 12
N_FAR, N_NEAR, N_Y, N_C, N_X = 8, 2, 4, 2, 4
PLANE = ("x", "near", "y", "c")
LOCAL = N_NEAR * N_Y * N_C
GROUP = N_FAR // N_X
F32 = jnp.float32
BF16 = jnp.bfloat16


def dot(left, right, contract, batch=((), ())):
    return lax.dot_general(left, right, (contract, batch), preferred_element_type=F32)


def shift(value, by):
    return lax.ppermute(value, "x", [(i, (i + by) % N_X) for i in range(N_X)])


def gather_x(value, me):
    whole = jnp.zeros((N_X,) + value.shape, value.dtype)
    for by in range(N_X):
        piece = value if by == 0 else shift(value, by)
        whole = lax.dynamic_update_slice_in_dim(whole, piece[None], (me - by) % N_X, 0)
    return whole


def plan(routes, gates, me_far):
    tok, top = routes.shape
    mine = jnp.concatenate([routes.T.astype(F32), gates.T], axis=0)
    every = lax.all_to_all(
        jnp.broadcast_to(mine[None], (N_FAR,) + mine.shape), "far", split_axis=0, concat_axis=0, tiled=True
    )
    named = every[:, :top].reshape(N_FAR, top, 1, tok)
    weight = every[:, top:].reshape(N_FAR, top, 1, tok)
    wanted = (me_far * LOCAL + jnp.arange(LOCAL, dtype=jnp.int32)).astype(F32)
    hit = named == wanted[None, None, :, None]
    member = jnp.sum(hit.astype(F32), axis=1)
    gate = jnp.sum(jnp.where(hit, weight, 0.0), axis=1)
    before = (jnp.arange(tok)[:, None] < jnp.arange(tok)[None, :]).astype(BF16)
    rank = dot(member.astype(BF16), before, ((2,), (0,)))
    within = (jnp.arange(N_FAR) % GROUP * MOST).astype(F32)
    slot = jnp.where(member > 0.5, rank + within[:, None, None], -1.0)

    def by_group(value):
        value = value.reshape(N_X, GROUP, LOCAL, tok)
        return value.transpose(0, 2, 1, 3).reshape(N_X, LOCAL, 1, GROUP * tok)

    slots = GROUP * MOST
    pick = by_group(slot) == jnp.arange(slots, dtype=jnp.int32).astype(F32)[None, None, :, None]
    row_gate = jnp.sum(jnp.where(pick, by_group(gate), 0.0), axis=3)
    return (
        pick.astype(BF16).reshape(N_X, LOCAL * slots, GROUP * tok),
        row_gate.reshape(N_X, LOCAL * slots, 1),
    )


def expert_kernel(rows, both_in, down, row_grad, hidden, d_gate, d_up, pre_gate, pre_up, back):
    step = pl.program_id(0)
    width, cols = down.shape[1:]

    @pl.when(step == 0)
    def _():
        pre_gate[...] = jnp.zeros_like(pre_gate)
        pre_up[...] = jnp.zeros_like(pre_up)
        back[...] = jnp.zeros_like(back)

    ins = rows[0, :, :cols]
    pre_gate[...] += dot(ins, both_in[step, :, :width], ((1,), (0,)))
    pre_up[...] += dot(ins, both_in[step, :, width:], ((1,), (0,)))
    back[...] += dot(rows[0, :, cols:], down[0], ((1,), (1,)))

    @pl.when(step == N_X - 1)
    def _():
        g, u, b = pre_gate[...], pre_up[...], back[...]
        s = jax.nn.sigmoid(g)
        activated = g * s
        hidden[...] = (activated * u).astype(BF16)
        du = (b * activated).astype(BF16)
        dg = (b * u * s * (1.0 + g * (1.0 - s))).astype(BF16)
        d_up[...] = du
        d_gate[...] = dg
        for j in range(N_X):
            from_gate = dot(dg, both_in[j, :, :width], ((1,), (1,)))
            from_up = dot(du, both_in[j, :, width:], ((1,), (1,)))
            row_grad[j] = (from_gate + from_up).astype(BF16)


def expert(rows, both_in, down):
    parts, count, both = rows.shape
    width, cols = down.shape[1:]
    whole = lambda shape: pl.BlockSpec(shape, lambda j: (0,) * len(shape))
    square = pltpu.HBM((count, width), BF16)
    return pl.pallas_call(
        expert_kernel,
        grid=(parts,),
        in_specs=[
            pl.BlockSpec((1, count, both), lambda j: (j, 0, 0)),
            whole(both_in.shape),
            pl.BlockSpec((1, width, cols), lambda j: (j, 0, 0)),
        ],
        out_specs=[whole((parts, count, cols)), *[whole((count, width))] * 3],
        out_shape=[pltpu.HBM((parts, count, cols), BF16), square, square, square],
        scratch_shapes=[pltpu.VMEM((count, width), F32)] * 3,
        compiler_params=pltpu.CompilerParams(
            dimension_semantics=("arbitrary",), vmem_limit_bytes=32 * 1024 * 1024
        ),
        cost_estimate=pl.CostEstimate(
            flops=10 * parts * count * cols * width, bytes_accessed=11_000_000, transcendentals=count * width
        ),
    )(rows, both_in, down)


def tokens_kernel(pick, back, out):
    tok = out.shape[1]
    for far in range(N_FAR):
        group, within = divmod(far, GROUP)
        chosen = pick[group, :, tok * within : tok * (within + 1)]
        out[far] = dot(chosen, back[group], ((0,), (0,))).astype(BF16)


def token_parts(pick, back):
    tok = pick.shape[2] // GROUP
    shape = N_FAR, tok, back.shape[2]
    return pl.pallas_call(
        tokens_kernel,
        out_shape=pltpu.HBM(shape, BF16),
        compiler_params=pltpu.CompilerParams(vmem_limit_bytes=32 * 1024 * 1024),
        cost_estimate=pl.CostEstimate(
            flops=2 * back.size * tok * GROUP, bytes_accessed=4_000_000, transcendentals=0
        ),
    )(pick, back)


def shards(tokens, grad_out, routes, gates, w_gate, w_up, w_down):
    me_far, me_x = lax.axis_index("far"), lax.axis_index("x")
    tok, cols = tokens.shape
    both = jnp.concatenate([tokens, grad_out], axis=1)
    both, w_gate, w_up, w_down = lax.optimization_barrier((both, w_gate[0], w_up[0], w_down[0]))
    column = lax.all_gather(both, "far", axis=0, tiled=True).reshape(N_X, GROUP * tok, 2 * cols)
    pick, row_gate = plan(routes, gates, me_far)
    full_in = gather_x(jnp.concatenate([w_gate, w_up], axis=1), me_x)
    full_down = gather_x(w_down, me_x)
    column, full_in, full_down = lax.optimization_barrier((column, full_in, full_down))

    rows = dot(pick, column, ((2,), (1,)), ((0,), (0,)))
    scale = jnp.where(jnp.arange(2 * cols)[None, None, :] < cols, 1.0, row_gate)
    rows = (rows * scale).astype(BF16)
    count = rows.shape[1]
    slots = count // LOCAL
    rows = lax.all_to_all(
        rows.reshape(-1, slots, 2 * cols), PLANE, split_axis=0, concat_axis=0, tiled=True
    ).reshape(N_X, count, 2 * cols)
    inputs, scaled = rows[:, :, :cols], rows[:, :, cols:]
    row_grad, hidden, d_gate, d_up = expert(rows, full_in, full_down)
    came_back = lax.all_to_all(
        row_grad.reshape(-1, slots, cols), PLANE, split_axis=0, concat_axis=0, tiled=True
    ).reshape(N_X, count, cols)
    d_tokens = lax.psum_scatter(token_parts(pick, came_back), "far", scatter_dimension=0)

    totals = [None, None, None]
    for by in (1, 3, 2, 0):
        to = (me_x + by) % N_X
        ins = lax.dynamic_index_in_dim(inputs, to, 0, keepdims=False)
        outs = lax.dynamic_index_in_dim(scaled, to, 0, keepdims=False)
        for k, (left, right) in enumerate(((ins, d_gate), (ins, d_up), (hidden, outs))):
            part = dot(left, right, ((0,), (0,))).astype(BF16)
            part = (shift(part, by) if by else part).astype(F32)
            totals[k] = part if totals[k] is None else totals[k] + part
    grads = [total.astype(BF16)[None] for total in totals]
    return (d_tokens, *grads)


def solution(mesh):
    sizes = (N_FAR, N_NEAR, N_Y, N_C, N_X)
    fine = Mesh(mesh.devices.reshape(sizes), ("far", "near", "y", "c", "x"))
    expert_axes = ("far", "near", "y", "c")
    return jax.shard_map(
        shards,
        mesh=fine,
        in_specs=(
            P(expert_axes, "x"),
            P(expert_axes, "x"),
            P(expert_axes, None),
            P(expert_axes, None),
            P(expert_axes, "x", None),
            P(expert_axes, "x", None),
            P(expert_axes, None, "x"),
        ),
        out_specs=(
            P(expert_axes, "x"),
            P(expert_axes, "x", None),
            P(expert_axes, "x", None),
            P(expert_axes, None, "x"),
        ),
        check_vma=False,
    )
```

```python
import jax
import jax.numpy as jnp
from jax import lax
from jax.experimental import pallas as pl
from jax.experimental.pallas import tpu as pltpu
from jax.sharding import Mesh
from jax.sharding import PartitionSpec as P

MOST = 12
N_FAR, N_NEAR, N_Y, N_C, N_X = 8, 2, 4, 2, 4
PLANE = ("x", "near", "y", "c")
LOCAL = N_NEAR * N_Y * N_C
GROUP = N_FAR // N_X
F32 = jnp.float32
BF16 = jnp.bfloat16


def dot(left, right, contract, batch=((), ())):
    return lax.dot_general(left, right, (contract, batch), preferred_element_type=F32)


def shift(value, by):
    return lax.ppermute(value, "x", [(i, (i + by) % N_X) for i in range(N_X)])


def gather_x(value, me):
    whole = jnp.zeros((N_X,) + value.shape, value.dtype)
    for by in range(N_X):
        piece = value if by == 0 else shift(value, by)
        whole = lax.dynamic_update_slice_in_dim(whole, piece[None], (me - by) % N_X, 0)
    return whole


def plan(routes, gates, me_far):
    tok, top = routes.shape
    mine = jnp.concatenate([routes.T.astype(F32), gates.T], axis=0)
    every = lax.all_to_all(
        jnp.broadcast_to(mine[None], (N_FAR,) + mine.shape), "far", split_axis=0, concat_axis=0, tiled=True
    )
    named = every[:, :top].reshape(N_FAR, top, 1, tok)
    weight = every[:, top:].reshape(N_FAR, top, 1, tok)
    wanted = (me_far * LOCAL + jnp.arange(LOCAL, dtype=jnp.int32)).astype(F32)
    hit = named == wanted[None, None, :, None]
    member = jnp.sum(hit.astype(F32), axis=1)
    gate = jnp.sum(jnp.where(hit, weight, 0.0), axis=1)
    before = (jnp.arange(tok)[:, None] < jnp.arange(tok)[None, :]).astype(BF16)
    rank = dot(member.astype(BF16), before, ((2,), (0,)))
    within = (jnp.arange(N_FAR) % GROUP * MOST).astype(F32)
    slot = jnp.where(member > 0.5, rank + within[:, None, None], -1.0)

    def by_group(value):
        value = value.reshape(N_X, GROUP, LOCAL, tok)
        return value.transpose(0, 2, 1, 3).reshape(N_X, LOCAL, 1, GROUP * tok)

    slots = GROUP * MOST
    pick = by_group(slot) == jnp.arange(slots, dtype=jnp.int32).astype(F32)[None, None, :, None]
    row_gate = jnp.sum(jnp.where(pick, by_group(gate), 0.0), axis=3)
    return (
        pick.astype(BF16).reshape(N_X, LOCAL * slots, GROUP * tok),
        row_gate.reshape(N_X, LOCAL * slots, 1),
    )


def expert_kernel(rows, both_in, down, row_grad, hidden, d_gate, d_up, pre_gate, pre_up, back):
    step = pl.program_id(0)
    width, cols = down.shape[1:]

    @pl.when(step == 0)
    def _():
        pre_gate[...] = jnp.zeros_like(pre_gate)
        pre_up[...] = jnp.zeros_like(pre_up)
        back[...] = jnp.zeros_like(back)

    ins = rows[0, :, :cols]
    pre_gate[...] += dot(ins, both_in[step, :, :width], ((1,), (0,)))
    pre_up[...] += dot(ins, both_in[step, :, width:], ((1,), (0,)))
    back[...] += dot(rows[0, :, cols:], down[0], ((1,), (1,)))

    @pl.when(step == N_X - 1)
    def _():
        g, u, b = pre_gate[...], pre_up[...], back[...]
        s = jax.nn.sigmoid(g)
        activated = g * s
        hidden[...] = (activated * u).astype(BF16)
        du = (b * activated).astype(BF16)
        dg = (b * u * s * (1.0 + g * (1.0 - s))).astype(BF16)
        d_up[...] = du
        d_gate[...] = dg
        for j in range(N_X):
            from_gate = dot(dg, both_in[j, :, :width], ((1,), (1,)))
            from_up = dot(du, both_in[j, :, width:], ((1,), (1,)))
            row_grad[j] = (from_gate + from_up).astype(BF16)


def expert(rows, both_in, down):
    parts, count, both = rows.shape
    width, cols = down.shape[1:]
    whole = lambda shape: pl.BlockSpec(shape, lambda j: (0,) * len(shape))
    square = pltpu.HBM((count, width), BF16)
    return pl.pallas_call(
        expert_kernel,
        grid=(parts,),
        in_specs=[
            pl.BlockSpec((1, count, both), lambda j: (j, 0, 0)),
            whole(both_in.shape),
            pl.BlockSpec((1, width, cols), lambda j: (j, 0, 0)),
        ],
        out_specs=[whole((parts, count, cols)), *[whole((count, width))] * 3],
        out_shape=[pltpu.HBM((parts, count, cols), BF16), square, square, square],
        scratch_shapes=[pltpu.VMEM((count, width), F32)] * 3,
        compiler_params=pltpu.CompilerParams(
            dimension_semantics=("arbitrary",), vmem_limit_bytes=32 * 1024 * 1024
        ),
        cost_estimate=pl.CostEstimate(
            flops=10 * parts * count * cols * width, bytes_accessed=11_000_000, transcendentals=count * width
        ),
    )(rows, both_in, down)


def tokens_kernel(pick, back, out):
    tok = out.shape[1]
    for u in range(GROUP):
        chosen = pick[0, :, tok * u : tok * (u + 1)]
        out[u] = dot(chosen, back[0], ((0,), (0,))).astype(BF16)


def token_parts(pick, back):
    groups, count, toks = pick.shape
    cols = back.shape[2]
    grouped = lambda *shape: pl.BlockSpec(shape, lambda i: (i, 0, 0))
    return pl.pallas_call(
        tokens_kernel,
        grid=(groups,),
        in_specs=[grouped(1, count, toks), grouped(1, count, cols)],
        out_specs=grouped(GROUP, toks // GROUP, cols),
        out_shape=pltpu.HBM((N_FAR, toks // GROUP, cols), BF16),
        compiler_params=pltpu.CompilerParams(
            dimension_semantics=("arbitrary",), vmem_limit_bytes=32 * 1024 * 1024
        ),
        cost_estimate=pl.CostEstimate(
            flops=2 * back.size * toks, bytes_accessed=4_000_000, transcendentals=0
        ),
    )(pick, back)


def shards(tokens, grad_out, routes, gates, w_gate, w_up, w_down):
    me_far, me_x = lax.axis_index("far"), lax.axis_index("x")
    tok, cols = tokens.shape
    both = jnp.concatenate([tokens, grad_out], axis=1)
    both, w_gate, w_up, w_down = lax.optimization_barrier((both, w_gate[0], w_up[0], w_down[0]))
    column = lax.all_gather(both, "far", axis=0, tiled=True).reshape(N_X, GROUP * tok, 2 * cols)
    pick, row_gate = plan(routes, gates, me_far)
    full_in = gather_x(jnp.concatenate([w_gate, w_up], axis=1), me_x)
    full_down = gather_x(w_down, me_x)
    column, full_in, full_down = lax.optimization_barrier((column, full_in, full_down))

    rows = dot(pick, column, ((2,), (1,)), ((0,), (0,)))
    scale = jnp.where(jnp.arange(2 * cols)[None, None, :] < cols, 1.0, row_gate)
    rows = (rows * scale).astype(BF16)
    count = rows.shape[1]
    slots = count // LOCAL
    rows = lax.all_to_all(
        rows.reshape(-1, slots, 2 * cols), PLANE, split_axis=0, concat_axis=0, tiled=True
    ).reshape(N_X, count, 2 * cols)
    inputs, scaled = rows[:, :, :cols], rows[:, :, cols:]
    row_grad, hidden, d_gate, d_up = expert(rows, full_in, full_down)
    came_back = lax.all_to_all(
        row_grad.reshape(-1, slots, cols), PLANE, split_axis=0, concat_axis=0, tiled=True
    ).reshape(N_X, count, cols)
    d_tokens = lax.psum_scatter(token_parts(pick, came_back), "far", scatter_dimension=0)

    totals = [None, None, None]
    for by in (1, 3, 2, 0):
        to = (me_x + by) % N_X
        ins = lax.dynamic_index_in_dim(inputs, to, 0, keepdims=False)
        outs = lax.dynamic_index_in_dim(scaled, to, 0, keepdims=False)
        for k, (left, right) in enumerate(((ins, d_gate), (ins, d_up), (hidden, outs))):
            part = dot(left, right, ((0,), (0,))).astype(BF16)
            part = (shift(part, by) if by else part).astype(F32)
            totals[k] = part if totals[k] is None else totals[k] + part
    grads = [total.astype(BF16)[None] for total in totals]
    return (d_tokens, *grads)


def solution(mesh):
    sizes = (N_FAR, N_NEAR, N_Y, N_C, N_X)
    fine = Mesh(mesh.devices.reshape(sizes), ("far", "near", "y", "c", "x"))
    expert_axes = ("far", "near", "y", "c")
    return jax.shard_map(
        shards,
        mesh=fine,
        in_specs=(
            P(expert_axes, "x"),
            P(expert_axes, "x"),
            P(expert_axes, None),
            P(expert_axes, None),
            P(expert_axes, "x", None),
            P(expert_axes, "x", None),
            P(expert_axes, None, "x"),
        ),
        out_specs=(
            P(expert_axes, "x"),
            P(expert_axes, "x", None),
            P(expert_axes, "x", None),
            P(expert_axes, None, "x"),
        ),
        check_vma=False,
    )
```
